1024 devices in a mesh: task: 32 (over z_hi, y, x), integ: 32 (over z_lo, core).
Axes of the slice: x: 4, y: 4, z: 32 (z_hi: 2, z_lo: 16; z = z_hi * 16 + z_lo), core: 2. Of those that a mesh axis runs over, the one named last changes fastest.
Arguments:
- amplitudes: bfloat16 [4096, 98304], P('integ', 'task'), may hold values from -6 to 6
- integrals: bfloat16 [98304, 1024], P(('task', 'integ')), may hold values from -0.0546875 to 0.0546875
- block_mask: int32 [768, 8], replicated, may hold values from 0 to 1, as said below
- residual_in: float32 [4096, 1024], P(('integ', 'task')), may hold values from -6 to 6
Outputs:
- residual_out: float32 [4096, 1024], P(('integ', 'task'))
The draws below stay inside these ranges and needn't reach their ends.
Inputs may be any that keep to these rules, and one draw needn't show every extreme that they name: block_mask[k, b] is 1 exactly when block k and block b carry the same one of 8 symmetry labels; every label carried by a residual block is carried by exactly 2 residual blocks, so a row of block_mask holds 0 or 2 ones.
All inputs are finite; a program needn't handle non-finite values.
Results may differ from the reference program's by a relative error of at most 0.0003.
Values may be sent and summed in bfloat16 or wider, within the bound.
No kernel may reach another device: no remote copies, remote signals or barrier semaphores. Data moves between devices by JAX's collectives and lax.ppermute only.
A program may use at most 32 MiB of HBM per device.

```python
import jax
import jax.numpy as jnp

TILE = 128
AB_TILES = 8
CD = 98304
CD_TILES = 768
AB = 1024
PAIRS = 4096


def draw_block_mask(key, part):
    key = jax.random.fold_in(key, 11)
    key_perm, key_pick, key_out, key_bias = jax.random.split(key, 4)
    labels = jax.random.permutation(key_perm, 8).astype(jnp.int32)
    half = AB_TILES // 2
    onehot_ab = (jnp.arange(AB_TILES)[:, None] // 2 == jnp.arange(8)[None, :]).astype(jnp.int32)
    ab_label = jnp.sum(onehot_ab * labels[None, :], axis=1)
    pick_in = jax.random.randint(key_pick, (CD_TILES,), 0, half)
    pick_out = half + jax.random.randint(key_out, (CD_TILES,), 0, 8 - half)
    bias = jax.random.randint(key_bias, (CD_TILES,), 0, CD_TILES)
    chosen = jnp.where(bias < jnp.arange(CD_TILES), pick_in, pick_out)
    onehot_cd = (chosen[:, None] == jnp.arange(8)[None, :]).astype(jnp.int32)
    cd_label = jnp.sum(onehot_cd * labels[None, :], axis=1)
    return (cd_label[:, None] == ab_label[None, :]).astype(jnp.int32)


def shard_levels(rng, extent, shards, smallest, high):
    factor_of = 1.0
    for position, shards_of in shards:
        draws = jax.random.uniform(jax.random.fold_in(jax.random.fold_in(rng, 6), position), (shards_of,), jnp.float32, smallest / len(shards), high / len(shards))
        factor_of = factor_of * jnp.repeat(jnp.exp(draws), extent[position] // shards_of).reshape((-1,) + (1,) * (len(extent) - 1 - position))
    return factor_of


def scatter_about(stream_key, shape, spread, bound, cuts=(), kind=jnp.bfloat16):
    values = jax.random.normal(stream_key, shape, jnp.float32) * spread
    if len(cuts) > 0:
        values = shard_levels(stream_key, shape, cuts, -0.22, 0.18) * values
    return jnp.clip(values, min=-bound, max=bound).astype(kind)


def setup_inputs(seed: int = 0) -> dict:
    key_of = jax.random.split(jax.random.key(seed), 5)
    amplitudes = scatter_about(key_of[0], (PAIRS, CD), 1.0, 6.0, ((0, 32), (1, 32)))
    integrals = scatter_about(key_of[1], (CD, AB), (CD // 8) ** -0.5, 0.0546875, ((0, 1024),))
    block_mask = draw_block_mask(jax.random.fold_in(key_of[4], 71), 0)
    residual_in = scatter_about(key_of[3], (PAIRS, AB), 1.0, 6.0, ((0, 1024),), jnp.float32)
    return dict(amplitudes=amplitudes, integrals=integrals, block_mask=block_mask, residual_in=residual_in)


def reference(amplitudes, integrals, block_mask, residual_in):
    expanded = jnp.repeat(jnp.repeat(block_mask, TILE, axis=0), TILE, axis=1)
    masked = integrals * expanded.astype(integrals.dtype)
    ladder = jnp.dot(amplitudes, masked, preferred_element_type=jnp.float32)
    return residual_in + 0.5 * ladder
```

```python
import jax
import jax.numpy as jnp
from jax import lax
from jax.experimental import pallas as pl
from jax.experimental.pallas import tpu as pltpu
from jax.sharding import Mesh
from jax.sharding import PartitionSpec as P

TILE = 128
ROWS = 96
GROUP = 32
TASK = ("zh", "y", "x")
INTEG = ("z8", "z4", "z2", "z1", "c")
SIZES = (2, 4, 4, 2, 2, 2, 2, 2)
GATHERS = ("z8", "z4", ("z2", "z1"))
SWAP = ((0, 1), (1, 0))


def chip_of(slot):
    z2, z1, z4, z8 = (slot >> 3) & 1, (slot >> 2) & 1, (slot >> 1) & 1, slot & 1
    return z8 * 8 + z4 * 4 + z2 * 2 + z1


def blocks_of(mask, tile):
    first, second, count = jnp.int32(0), jnp.int32(0), jnp.int32(0)
    for b in range(8):
        one = mask[tile, b] != 0
        first = jnp.where(one & (count == 0), b, first)
        second = jnp.where(one & (count == 1), b, second)
        count = count + one.astype(jnp.int32)
    return first, second, count


def block_cols(block):
    return pl.ds(pl.multiple_of(block * TILE, TILE), TILE)


def fetch_mask(mask_hbm, mask, sem):
    tiles = mask.shape[0]
    task = lax.axis_index(TASK)
    copy = pltpu.make_async_copy(mask_hbm.at[pl.ds(pl.multiple_of(task * tiles, 8), tiles)], mask, sem)
    copy.start()
    copy.wait()


def compress_kernel(mask_hbm, rows_ref, out_ref, mask, sem):
    fetch_mask(mask_hbm, mask, sem)
    integ = lax.axis_index(INTEG)
    for g in range(ROWS // GROUP):
        tile = (integ * ROWS + g * GROUP) // TILE
        first, second, count = blocks_of(mask, tile)
        rows = pl.ds(g * GROUP, GROUP)
        for half, block in ((0, first), (1, second)):
            part = rows_ref[rows, block_cols(block)]
            out_ref[rows, pl.ds(half * TILE, TILE)] = jnp.where(count > half, part, jnp.zeros_like(part))


def ladder_kernel(mask_hbm, amp_ref, own_ref, other_ref, out_ref, mask, packed, total, sem):
    fetch_mask(mask_hbm, mask, sem)
    core = lax.axis_index("c")
    for slot in range(16):
        rows = pl.ds(slot * ROWS, ROWS)
        for which, ref in ((core, own_ref), (1 - core, other_ref)):
            at = pl.multiple_of((2 * chip_of(slot) + which) * ROWS, GROUP)
            packed[pl.ds(at, ROWS), :] = ref[rows, :]
    total[...] = jnp.zeros_like(total)
    for tile in range(mask.shape[0]):
        first, second, _ = blocks_of(mask, tile)
        cols = pl.ds(tile * TILE, TILE)
        part = jnp.dot(amp_ref[:, cols], packed[cols, :], preferred_element_type=jnp.float32)
        total[:, block_cols(first)] += part[:, :TILE]
        total[:, block_cols(second)] += part[:, TILE:]
    largest = jnp.max(jnp.abs(total[...]))
    exponent = jnp.floor(jnp.log2(jnp.maximum(jnp.full((8, TILE), largest), 2.0**-100))) - 10.0
    width = total.shape[1]
    out_ref[:, :width] = (total[...] * (0.5 * jnp.exp2(-exponent[:1, :1]))).astype(out_ref.dtype)
    out_ref[:, width:] = jnp.broadcast_to(exponent[:1], (total.shape[0], TILE)).astype(out_ref.dtype)


def combine_kernel(parts_ref, residual_ref, out_ref):
    width = out_ref.shape[1]
    total = residual_ref[...]
    for task in range(parts_ref.shape[0]):
        scale = jnp.exp2(parts_ref[task, :, width:].astype(jnp.float32))
        total = total + parts_ref[task, :, :width].astype(jnp.float32) * scale[:, :1]
    out_ref[...] = total


def per_device(amplitudes, integrals, block_mask, residual_in):
    cd_tiles, ab_tiles = block_mask.shape
    pairs, width = amplitudes.shape[0], ab_tiles * TILE
    tasks = lax.axis_size(TASK)
    tiles = cd_tiles // tasks
    any_spec = pl.BlockSpec(memory_space=pl.ANY)
    vmem_spec = pl.BlockSpec(memory_space=pltpu.VMEM)
    packed = pl.pallas_call(
        compress_kernel,
        out_shape=jax.ShapeDtypeStruct((ROWS, 2 * TILE), jnp.bfloat16),
        in_specs=[any_spec, vmem_spec],
        out_specs=vmem_spec,
        scratch_shapes=[pltpu.SMEM((tiles, ab_tiles), jnp.int32), pltpu.SemaphoreType.DMA],
        name="compress",
    )(block_mask, integrals)
    for axis in GATHERS:
        packed = lax.all_gather(packed, axis, axis=0, tiled=True)
    other = lax.ppermute(packed, "c", SWAP)
    ladder = pl.pallas_call(
        ladder_kernel,
        out_shape=jax.ShapeDtypeStruct((pairs, width + TILE), jnp.float32),
        in_specs=[any_spec] + [vmem_spec] * 3,
        out_specs=vmem_spec,
        scratch_shapes=[
            pltpu.SMEM((tiles, ab_tiles), jnp.int32),
            pltpu.VMEM((32 * ROWS, 2 * TILE), jnp.bfloat16),
            pltpu.VMEM((pairs, width), jnp.float32),
            pltpu.SemaphoreType.DMA,
        ],
        compiler_params=pltpu.CompilerParams(vmem_limit_bytes=32 * 1024 * 1024),
        name="ladder",
    )(block_mask, amplitudes, packed, other)
    messages = ladder.astype(jnp.float16).reshape(tasks, pairs // tasks, width + TILE)
    parts = lax.all_to_all(messages, TASK, 0, 0, tiled=True).astype(jnp.float32)
    return pl.pallas_call(
        combine_kernel,
        out_shape=jax.ShapeDtypeStruct(residual_in.shape, jnp.float32),
        in_specs=[vmem_spec] * 2,
        out_specs=vmem_spec,
        name="combine",
    )(parts, residual_in)


def solution(mesh):
    fine = Mesh(mesh.devices.reshape(SIZES), TASK + INTEG)
    return jax.shard_map(
        per_device,
        mesh=fine,
        in_specs=(P(INTEG, TASK), P(TASK + INTEG, None), P(), P(INTEG + TASK, None)),
        out_specs=P(INTEG + TASK, None),
        check_vma=False,
    )
```

```python
import functools

import jax
import jax.numpy as jnp
from jax import lax
from jax.experimental import pallas as pl
from jax.experimental.pallas import tpu as pltpu
from jax.sharding import Mesh
from jax.sharding import PartitionSpec as P

TILE = 128
ROWS = 96
GROUP = 32
TASK = ("zh", "y", "x")
PLANE = ("y", "x")
INTEG = ("z8", "z4", "z2", "z1", "c")
SIZES = (2, 4, 4, 2, 2, 2, 2, 2)
SWAP = ((0, 1), (1, 0))


def chip_of(slot):
    z2, z1, z4 = (slot >> 2) & 1, (slot >> 1) & 1, slot & 1
    return z4 * 4 + z2 * 2 + z1


def blocks_of(mask, tile):
    first, second, count = jnp.int32(0), jnp.int32(0), jnp.int32(0)
    for b in range(mask.shape[0]):
        one = mask[b, tile] != 0
        first = jnp.where(one & (count == 0), b, first)
        second = jnp.where(one & (count == 1), b, second)
        count = count + one.astype(jnp.int32)
    return first, second, count


def block_cols(block):
    return pl.ds(pl.multiple_of(block * TILE, TILE), TILE)


def compress_kernel(tiles, mask, rows_ref, out_ref):
    task, integ = lax.axis_index(TASK), lax.axis_index(INTEG)
    for g in range(ROWS // GROUP):
        tile = task * tiles + (integ * ROWS + g * GROUP) // TILE
        first, second, count = blocks_of(mask, tile)
        rows = pl.ds(g * GROUP, GROUP)
        for half, block in ((0, first), (1, second)):
            part = rows_ref[rows, block_cols(block)]
            out_ref[rows, pl.ds(half * TILE, TILE)] = jnp.where(count > half, part, jnp.zeros_like(part))


def ladder_kernel(tiles, flip, mask, amp_ref, near_ref, near_swapped_ref, far_ref, after_ref, out_ref, packed, total):
    core, z8, zh = lax.axis_index("c"), lax.axis_index("z8"), lax.axis_index("zh")
    for slot in range(8):
        rows = pl.ds(slot * ROWS, ROWS)
        near, far = z8 * 8 + chip_of(slot), (1 - z8) * 8 + chip_of(slot)
        for chip, which, ref in ((near, core, near_ref), (near, 1 - core, near_swapped_ref)):
            packed[pl.ds(pl.multiple_of((2 * chip + which) * ROWS, GROUP), ROWS), :] = ref[rows, :]
        for which in range(2):
            at = pl.multiple_of((2 * far + which) * ROWS, GROUP)
            packed[pl.ds(at, ROWS), :] = far_ref[pl.ds((which * 8 + slot) * ROWS, ROWS), :]
    pairs, width = total.shape
    half = 1 - zh if flip else zh
    amp_rows = pl.ds(pl.multiple_of(half * pairs, pairs), pairs)
    total[...] = jnp.zeros_like(total)
    for tile in range(tiles):
        first, second, _ = blocks_of(mask, lax.axis_index(TASK) * tiles + tile)
        cols = pl.ds(tile * TILE, TILE)
        part = jnp.dot(amp_ref[amp_rows, cols], packed[cols, :], preferred_element_type=jnp.float32)
        total[:, block_cols(first)] += part[:, :TILE]
        total[:, block_cols(second)] += part[:, TILE:]
    largest = jnp.max(jnp.abs(total[...]))
    exponent = jnp.floor(jnp.log2(jnp.maximum(jnp.full((8, TILE), largest), 2.0**-100))) - 10.0
    out_ref[:, :width] = total[...] * (0.5 * jnp.exp2(-exponent[:1, :1]))
    out_ref[:, width:] = jnp.broadcast_to(exponent[:1], (pairs, TILE))


def combine_kernel(parts_ref, start_ref, out_ref):
    width = out_ref.shape[1]
    total = start_ref[...]
    for i in range(parts_ref.shape[0]):
        total = total + parts_ref[i, :, :width] * jnp.exp2(parts_ref[i, :, width:])[:, :1]
    out_ref[...] = total


def per_device(amplitudes, integrals, block_mask, residual_in):
    cd_tiles, ab_tiles = block_mask.shape
    pairs, width = amplitudes.shape[0] // 2, ab_tiles * TILE
    tiles = cd_tiles // lax.axis_size(TASK)
    places = lax.axis_size(PLANE)
    smem_spec = pl.BlockSpec(memory_space=pltpu.SMEM)
    vmem_spec = pl.BlockSpec(memory_space=pltpu.VMEM)
    mask = block_mask.T
    gather = functools.partial(lax.all_gather, axis=0, tiled=True)

    own = pl.pallas_call(
        functools.partial(compress_kernel, tiles),
        out_shape=jax.ShapeDtypeStruct((ROWS, 2 * TILE), jnp.bfloat16),
        in_specs=[smem_spec, vmem_spec],
        out_specs=vmem_spec,
        name="compress",
    )(mask, integrals)
    across = lax.ppermute(own, "z8", SWAP)
    near = gather(gather(own, "z4"), ("z2", "z1"))
    near_swapped = lax.ppermute(near, "c", SWAP)
    far = gather(gather(gather(across, "z4"), ("z2", "z1")), "c")

    def reduced(flip, start, after):
        ladder = pl.pallas_call(
            functools.partial(ladder_kernel, tiles, flip),
            out_shape=jax.ShapeDtypeStruct((pairs, width + TILE), jnp.float32),
            in_specs=[smem_spec] + [vmem_spec] * 4 + [pl.BlockSpec(memory_space=pl.ANY)],
            out_specs=vmem_spec,
            scratch_shapes=[
                pltpu.VMEM((32 * ROWS, 2 * TILE), jnp.bfloat16),
                pltpu.VMEM((pairs, width), jnp.float32),
            ],
            compiler_params=pltpu.CompilerParams(vmem_limit_bytes=32 * 1024 * 1024),
            name="ladder",
        )(mask, amplitudes, near, near_swapped, far, after)
        messages = ladder.astype(jnp.float16).reshape(places, pairs // places, width + TILE)
        parts = lax.all_to_all(messages, PLANE, 0, 0, tiled=True).astype(jnp.float32)
        return pl.pallas_call(
            combine_kernel,
            out_shape=jax.ShapeDtypeStruct(residual_in.shape, jnp.float32),
            in_specs=[vmem_spec] * 2,
            out_specs=vmem_spec,
            name="combine",
        )(parts, start)

    theirs = reduced(True, jnp.zeros_like(residual_in), mask)
    received = lax.ppermute(theirs, "zh", SWAP)
    return reduced(False, residual_in, theirs) + received


def solution(mesh):
    fine = Mesh(mesh.devices.reshape(SIZES), TASK + INTEG)
    return jax.shard_map(
        per_device,
        mesh=fine,
        in_specs=(P(INTEG, TASK), P(TASK + INTEG, None), P(), P(INTEG + TASK, None)),
        out_specs=P(INTEG + TASK, None),
        check_vma=False,
    )
```

```python
import functools

import jax
import jax.numpy as jnp
from jax import lax
from jax.experimental import pallas as pl
from jax.experimental.pallas import tpu as pltpu
from jax.sharding import Mesh
from jax.sharding import PartitionSpec as P

TILE = 128
ROWS = 96
GROUP = 32
TASK = ("zh", "y", "x")
PLANE = ("y", "x")
INTEG = ("z8", "z4", "z2", "z1", "c")
SIZES = (2, 4, 4, 2, 2, 2, 2, 2)
SWAP = ((0, 1), (1, 0))


def chip_of(slot, z8):
    z2, z1, across, z4 = (slot >> 3) & 1, (slot >> 2) & 1, (slot >> 1) & 1, slot & 1
    return (1 - z8 if across else z8) * 8 + z4 * 4 + z2 * 2 + z1


def blocks_of(mask, tile):
    first, second, count = jnp.int32(0), jnp.int32(0), jnp.int32(0)
    for b in range(mask.shape[0]):
        one = mask[b, tile] != 0
        first = jnp.where(one & (count == 0), b, first)
        second = jnp.where(one & (count == 1), b, second)
        count = count + one.astype(jnp.int32)
    return first, second, count


def block_cols(block):
    return pl.ds(pl.multiple_of(block * TILE, TILE), TILE)


def compress_kernel(tiles, mask, rows_ref, out_ref):
    task, integ = lax.axis_index(TASK), lax.axis_index(INTEG)
    for g in range(ROWS // GROUP):
        tile = task * tiles + (integ * ROWS + g * GROUP) // TILE
        first, second, count = blocks_of(mask, tile)
        rows = pl.ds(g * GROUP, GROUP)
        for half, block in ((0, first), (1, second)):
            part = rows_ref[rows, block_cols(block)]
            out_ref[rows, pl.ds(half * TILE, TILE)] = jnp.where(count > half, part, jnp.zeros_like(part))


def ladder_kernel(tiles, mask, amp_ref, own_ref, other_ref, out_ref, packed, total):
    core, z8 = lax.axis_index("c"), lax.axis_index("z8")
    for slot in range(16):
        rows = pl.ds(slot * ROWS, ROWS)
        for which, ref in ((core, own_ref), (1 - core, other_ref)):
            at = pl.multiple_of((2 * chip_of(slot, z8) + which) * ROWS, GROUP)
            packed[pl.ds(at, ROWS), :] = ref[rows, :]
    pairs, width = total.shape
    total[...] = jnp.zeros_like(total)
    for tile in range(tiles):
        first, second, _ = blocks_of(mask, lax.axis_index(TASK) * tiles + tile)
        cols = pl.ds(tile * TILE, TILE)
        part = jnp.dot(amp_ref[:, cols], packed[cols, :], preferred_element_type=jnp.float32)
        total[:, block_cols(first)] += part[:, :TILE]
        total[:, block_cols(second)] += part[:, TILE:]
    largest = jnp.max(jnp.abs(total[...]))
    exponent = jnp.floor(jnp.log2(jnp.maximum(jnp.full((8, TILE), largest), 2.0**-100))) - 10.0
    scale = 0.5 * jnp.exp2(-exponent[:1, :1])
    places, rows = out_ref.shape[0], out_ref.shape[1] // 2
    for place in range(places):
        for zh in range(2):
            piece = total[pl.ds((zh * places + place) * rows, rows), :]
            out_ref[place, pl.ds(zh * rows, rows), :width] = piece * scale
        out_ref[place, :, width:] = exponent


def combine_kernel(parts_ref, residual_ref, mine_ref, theirs_ref):
    rows, width = residual_ref.shape
    total = jnp.zeros((2 * rows, width), jnp.float32)
    for i in range(parts_ref.shape[0]):
        total = total + parts_ref[i, :, :width] * jnp.exp2(parts_ref[i, :, width:])[:, :1]
    first = lax.axis_index("zh") == 0
    mine_ref[...] = residual_ref[...] + jnp.where(first, total[:rows], total[rows:])
    theirs_ref[...] = jnp.where(first, total[rows:], total[:rows])


def per_device(amplitudes, integrals, block_mask, residual_in):
    cd_tiles, ab_tiles = block_mask.shape
    pairs, width = amplitudes.shape[0], ab_tiles * TILE
    tiles = cd_tiles // lax.axis_size(TASK)
    places = lax.axis_size(PLANE)
    smem_spec = pl.BlockSpec(memory_space=pltpu.SMEM)
    vmem_spec = pl.BlockSpec(memory_space=pltpu.VMEM)
    mask = block_mask.T
    gather = functools.partial(lax.all_gather, axis=0, tiled=True)

    messages = (places, 2 * residual_in.shape[0], width + TILE)
    packed = pl.pallas_call(
        functools.partial(compress_kernel, tiles),
        out_shape=jax.ShapeDtypeStruct((ROWS, 2 * TILE), jnp.bfloat16),
        in_specs=[smem_spec, vmem_spec],
        out_specs=vmem_spec,
        name="compress",
    )(mask, integrals)
    across = lax.ppermute(packed, "z8", SWAP)
    own = gather(jnp.concatenate([gather(packed, "z4"), gather(across, "z4")]), ("z2", "z1"))
    other = lax.ppermute(own, "c", SWAP)
    ladder = pl.pallas_call(
        functools.partial(ladder_kernel, tiles),
        out_shape=jax.ShapeDtypeStruct(messages, jnp.float32),
        in_specs=[smem_spec] + [vmem_spec] * 3,
        out_specs=vmem_spec,
        scratch_shapes=[
            pltpu.VMEM((32 * ROWS, 2 * TILE), jnp.bfloat16),
            pltpu.VMEM((pairs, width), jnp.float32),
        ],
        compiler_params=pltpu.CompilerParams(vmem_limit_bytes=32 * 1024 * 1024),
        name="ladder",
    )(mask, amplitudes, own, other)
    parts = lax.all_to_all(ladder.astype(jnp.float16), PLANE, 0, 0, tiled=True)
    mine, theirs = pl.pallas_call(
        combine_kernel,
        out_shape=(jax.ShapeDtypeStruct(residual_in.shape, jnp.float32),) * 2,
        in_specs=[vmem_spec] * 2,
        out_specs=(vmem_spec, vmem_spec),
        name="combine",
    )(parts.astype(jnp.float32), residual_in)
    return mine + lax.ppermute(theirs, "zh", SWAP)


def solution(mesh):
    fine = Mesh(mesh.devices.reshape(SIZES), TASK + INTEG)
    return jax.shard_map(
        per_device,
        mesh=fine,
        in_specs=(P(INTEG, TASK), P(TASK + INTEG, None), P(), P(INTEG + TASK, None)),
        out_specs=P(INTEG + TASK, None),
        check_vma=False,
    )
```

```python
import functools

import jax
import jax.numpy as jnp
from jax import lax
from jax.experimental import pallas as pl
from jax.experimental.pallas import tpu as pltpu
from jax.sharding import Mesh
from jax.sharding import PartitionSpec as P

TILE = 128
ROWS = 96
GROUP = 32
TASK = ("zh", "y", "x")
PLANE = ("y", "x")
INTEG = ("z8", "z4", "z2", "z1", "c")
SIZES = (2, 4, 4, 2, 2, 2, 2, 2)
SWAP = ((0, 1), (1, 0))
MIB = 1024 * 1024


def chip_of(slot):
    z2, z1, z4, z8 = (slot >> 3) & 1, (slot >> 2) & 1, (slot >> 1) & 1, slot & 1
    return z8 * 8 + z4 * 4 + z2 * 2 + z1


def blocks_of(mask, tile):
    first, second, count = jnp.int32(0), jnp.int32(0), jnp.int32(0)
    for b in range(mask.shape[0]):
        one = mask[b, tile] != 0
        first = jnp.where(one & (count == 0), b, first)
        second = jnp.where(one & (count == 1), b, second)
        count = count + one.astype(jnp.int32)
    return first, second, count


def block_cols(block):
    return pl.ds(pl.multiple_of(block * TILE, TILE), TILE)


def compress_kernel(tiles, mask, rows_ref, out_ref):
    task, integ = lax.axis_index(TASK), lax.axis_index(INTEG)
    for g in range(ROWS // GROUP):
        tile = task * tiles + (integ * ROWS + g * GROUP) // TILE
        first, second, count = blocks_of(mask, tile)
        rows = pl.ds(g * GROUP, GROUP)
        for half, block in ((0, first), (1, second)):
            part = rows_ref[rows, block_cols(block)]
            out_ref[rows, pl.ds(half * TILE, TILE)] = jnp.where(count > half, part, jnp.zeros_like(part))


def ladder_kernel(tiles, mask, amp_ref, own_ref, other_ref, out_ref, packed, total):
    core = lax.axis_index("c")
    for slot in range(16):
        rows = pl.ds(slot * ROWS, ROWS)
        for which, ref in ((core, own_ref), (1 - core, other_ref)):
            at = pl.multiple_of((2 * chip_of(slot) + which) * ROWS, GROUP)
            packed[pl.ds(at, ROWS), :] = ref[rows, :]
    pairs, width = total.shape
    total[...] = jnp.zeros_like(total)
    for tile in range(tiles):
        first, second, _ = blocks_of(mask, lax.axis_index(TASK) * tiles + tile)
        cols = pl.ds(tile * TILE, TILE)
        part = jnp.dot(amp_ref[:, cols], packed[cols, :], preferred_element_type=jnp.float32)
        total[:, block_cols(first)] += part[:, :TILE]
        total[:, block_cols(second)] += part[:, TILE:]
    largest = jnp.max(jnp.abs(total[...]))
    exponent = jnp.floor(jnp.log2(jnp.maximum(jnp.full((8, TILE), largest), 2.0**-100))) - 10.0
    scale = 0.5 * jnp.exp2(-exponent[:1, :1])
    places, rows = out_ref.shape[0], out_ref.shape[1] // 2
    for place in range(places):
        for zh in range(2):
            piece = total[pl.ds((zh * places + place) * rows, rows), :]
            out_ref[place, pl.ds(zh * rows, rows), :width] = piece * scale
        out_ref[place, :, width:] = exponent


def combine_kernel(parts_ref, residual_ref, mine_ref, theirs_ref):
    rows, width = residual_ref.shape
    total = jnp.zeros((2 * rows, width), jnp.float32)
    for i in range(parts_ref.shape[0]):
        total = total + parts_ref[i, :, :width] * jnp.exp2(parts_ref[i, :, width:])[:, :1]
    first = lax.axis_index("zh") == 0
    mine_ref[...] = residual_ref[...] + jnp.where(first, total[:rows], total[rows:])
    theirs_ref[...] = jnp.where(first, total[rows:], total[:rows])


def per_device(amplitudes, integrals, block_mask, residual_in):
    cd_tiles, ab_tiles = block_mask.shape
    pairs, width = amplitudes.shape[0], ab_tiles * TILE
    tiles = cd_tiles // lax.axis_size(TASK)
    places = lax.axis_size(PLANE)
    smem_spec = pl.BlockSpec(memory_space=pltpu.SMEM)
    vmem_spec = pl.BlockSpec(memory_space=pltpu.VMEM)
    mask = block_mask.T
    gather = functools.partial(lax.all_gather, axis=0, tiled=True)

    messages = (places, 2 * residual_in.shape[0], width + TILE)
    packed = pl.pallas_call(
        functools.partial(compress_kernel, tiles),
        out_shape=jax.ShapeDtypeStruct((ROWS, 2 * TILE), jnp.bfloat16),
        in_specs=[smem_spec, vmem_spec],
        out_specs=vmem_spec,
        name="compress",
    )(mask, integrals)
    own = gather(gather(gather(packed, "z8"), "z4"), ("z2", "z1"))
    other = lax.ppermute(own, "c", SWAP)
    ladder = pl.pallas_call(
        functools.partial(ladder_kernel, tiles),
        out_shape=jax.ShapeDtypeStruct(messages, jnp.float32),
        in_specs=[smem_spec] + [vmem_spec] * 3,
        out_specs=vmem_spec,
        scratch_shapes=[
            pltpu.VMEM((32 * ROWS, 2 * TILE), jnp.bfloat16),
            pltpu.VMEM((pairs, width), jnp.float32),
        ],
        compiler_params=pltpu.CompilerParams(vmem_limit_bytes=12 * MIB),
        name="ladder",
    )(mask, amplitudes, own, other)
    parts = lax.all_to_all(ladder.astype(jnp.float16), PLANE, 0, 0, tiled=True)
    mine, theirs = pl.pallas_call(
        combine_kernel,
        out_shape=(jax.ShapeDtypeStruct(residual_in.shape, jnp.float32),) * 2,
        in_specs=[vmem_spec] * 2,
        out_specs=(vmem_spec, vmem_spec),
        compiler_params=pltpu.CompilerParams(vmem_limit_bytes=4 * MIB),
        name="combine",
    )(parts.astype(jnp.float32), residual_in)
    return mine + lax.ppermute(theirs, "zh", SWAP)


def solution(mesh):
    fine = Mesh(mesh.devices.reshape(SIZES), TASK + INTEG)
    return jax.shard_map(
        per_device,
        mesh=fine,
        in_specs=(P(INTEG, TASK), P(TASK + INTEG, None), P(), P(INTEG + TASK, None)),
        out_specs=P(INTEG + TASK, None),
        check_vma=False,
    )
```

```python
import functools

import jax
import jax.numpy as jnp
from jax import lax
from jax.experimental import pallas as pl
from jax.experimental.pallas import tpu as pltpu
from jax.sharding import Mesh
from jax.sharding import PartitionSpec as P

TILE = 128
ROWS = 96
GROUP = 32
TASK = ("zh", "y", "x")
PLANE = ("y", "x")
INTEG = ("z8", "z4", "z2", "z1", "c")
SIZES = (2, 4, 4, 2, 2, 2, 2, 2)
SWAP = ((0, 1), (1, 0))
MIB = 1024 * 1024


def chip_of(slot):
    z2, z1, z4, z8 = (slot >> 3) & 1, (slot >> 2) & 1, (slot >> 1) & 1, slot & 1
    return z8 * 8 + z4 * 4 + z2 * 2 + z1


def blocks_of(mask, tile):
    first, second, count = jnp.int32(0), jnp.int32(0), jnp.int32(0)
    for b in range(mask.shape[0]):
        one = mask[b, tile] != 0
        first = jnp.where(one & (count == 0), b, first)
        second = jnp.where(one & (count == 1), b, second)
        count = count + one.astype(jnp.int32)
    return first, second, count


def block_cols(block):
    return pl.ds(pl.multiple_of(block * TILE, TILE), TILE)


def compress_kernel(tiles, mask, rows_ref, out_ref):
    task, integ = lax.axis_index(TASK), lax.axis_index(INTEG)
    for g in range(ROWS // GROUP):
        tile = task * tiles + (integ * ROWS + g * GROUP) // TILE
        first, second, count = blocks_of(mask, tile)
        rows = pl.ds(g * GROUP, GROUP)
        for half, block in ((0, first), (1, second)):
            part = rows_ref[rows, block_cols(block)]
            out_ref[rows, pl.ds(half * TILE, TILE)] = jnp.where(count > half, part, jnp.zeros_like(part))


def ladder_kernel(tiles, mask, amp_ref, own_ref, other_ref, out_ref, packed, total):
    core = lax.axis_index("c")
    for slot in range(16):
        rows = pl.ds(slot * ROWS, ROWS)
        for which, ref in ((core, own_ref), (1 - core, other_ref)):
            at = pl.multiple_of((2 * chip_of(slot) + which) * ROWS, GROUP)
            packed[pl.ds(at, ROWS), :] = ref[rows, :]
    pairs, width = total.shape
    total[...] = jnp.zeros_like(total)
    for tile in range(tiles):
        first, second, _ = blocks_of(mask, lax.axis_index(TASK) * tiles + tile)
        cols = pl.ds(tile * TILE, TILE)
        part = jnp.dot(amp_ref[:, cols], packed[cols, :], preferred_element_type=jnp.float32)
        total[:, block_cols(first)] += part[:, :TILE]
        total[:, block_cols(second)] += part[:, TILE:]
    largest = jnp.max(jnp.abs(total[...]))
    exponent = jnp.floor(jnp.log2(jnp.maximum(jnp.full((8, TILE), largest), 2.0**-100))) - 10.0
    scale = 0.5 * jnp.exp2(-exponent[:1, :1])
    places, rows = out_ref.shape[0], out_ref.shape[1] // 2
    for place in range(places):
        for zh in range(2):
            piece = total[pl.ds((zh * places + place) * rows, rows), :]
            out_ref[place, pl.ds(zh * rows, rows), :width] = piece * scale
        out_ref[place, :, width:] = exponent


def combine_kernel(parts_ref, mine_ref, theirs_ref):
    rows, width = mine_ref.shape
    total = jnp.zeros((2 * rows, width), jnp.float32)
    for i in range(parts_ref.shape[0]):
        total = total + parts_ref[i, :, :width] * jnp.exp2(parts_ref[i, :, width:])[:, :1]
    first = lax.axis_index("zh") == 0
    mine_ref[...] = jnp.where(first, total[:rows], total[rows:])
    theirs_ref[...] = jnp.where(first, total[rows:], total[:rows])


def per_device(amplitudes, integrals, block_mask, residual_in):
    cd_tiles, ab_tiles = block_mask.shape
    pairs, width = amplitudes.shape[0], ab_tiles * TILE
    tiles = cd_tiles // lax.axis_size(TASK)
    places = lax.axis_size(PLANE)
    smem_spec = pl.BlockSpec(memory_space=pltpu.SMEM)
    vmem_spec = pl.BlockSpec(memory_space=pltpu.VMEM)
    mask = block_mask.T
    gather = functools.partial(lax.all_gather, axis=0, tiled=True)

    messages = (places, 2 * residual_in.shape[0], width + TILE)
    packed = pl.pallas_call(
        functools.partial(compress_kernel, tiles),
        out_shape=jax.ShapeDtypeStruct((ROWS, 2 * TILE), jnp.bfloat16),
        in_specs=[smem_spec, vmem_spec],
        out_specs=vmem_spec,
        name="compress",
    )(mask, integrals)
    own = gather(gather(gather(packed, "z8"), "z4"), ("z2", "z1"))
    other = lax.ppermute(own, "c", SWAP)
    ladder = pl.pallas_call(
        functools.partial(ladder_kernel, tiles),
        out_shape=jax.ShapeDtypeStruct(messages, jnp.float32),
        in_specs=[smem_spec] + [vmem_spec] * 3,
        out_specs=vmem_spec,
        scratch_shapes=[
            pltpu.VMEM((32 * ROWS, 2 * TILE), jnp.bfloat16),
            pltpu.VMEM((pairs, width), jnp.float32),
        ],
        compiler_params=pltpu.CompilerParams(vmem_limit_bytes=12 * MIB),
        name="ladder",
    )(mask, amplitudes, own, other)
    parts = lax.all_to_all(ladder.astype(jnp.float16), PLANE, 0, 0, tiled=True)
    mine, theirs = pl.pallas_call(
        combine_kernel,
        out_shape=(jax.ShapeDtypeStruct(residual_in.shape, jnp.float32),) * 2,
        in_specs=[vmem_spec],
        out_specs=(vmem_spec, vmem_spec),
        compiler_params=pltpu.CompilerParams(vmem_limit_bytes=4 * MIB),
        name="combine",
    )(parts.astype(jnp.float32))
    both = lax.all_gather(theirs, "zh", axis=0)
    return residual_in + (mine + jnp.where(lax.axis_index("zh") == 0, both[1], both[0]))


def solution(mesh):
    fine = Mesh(mesh.devices.reshape(SIZES), TASK + INTEG)
    return jax.shard_map(
        per_device,
        mesh=fine,
        in_specs=(P(INTEG, TASK), P(TASK + INTEG, None), P(), P(INTEG + TASK, None)),
        out_specs=P(INTEG + TASK, None),
        check_vma=False,
    )
```

```python
import functools

import jax
import jax.numpy as jnp
from jax import lax
from jax.experimental import pallas as pl
from jax.experimental.pallas import tpu as pltpu
from jax.sharding import Mesh
from jax.sharding import PartitionSpec as P

TILE = 128
ROWS = 96
GROUP = 32
TASK = ("zh", "y", "x")
PLANE = ("y", "x")
INTEG = ("z8", "z4", "z2", "z1", "c")
SIZES = (2, 4, 4, 2, 2, 2, 2, 2)
SWAP = ((0, 1), (1, 0))
RING = (0, 1, 3, 2)
WINDOW = 2 * TILE
MIB = 1024 * 1024


def chip_of(slot):
    return (slot & 1) * 8 + ((slot >> 1) & 1) * 4 + RING[slot >> 2]


def blocks_of(mask, tile):
    first, second, count = jnp.int32(0), jnp.int32(0), jnp.int32(0)
    for b in range(mask.shape[0]):
        one = mask[b, tile] != 0
        first = jnp.where(one & (count == 0), b, first)
        second = jnp.where(one & (count == 1), b, second)
        count = count + one.astype(jnp.int32)
    return first, second, count


def mask_copy(mask_hbm, mask, sem, tiles):
    tile = lax.axis_index(TASK) * tiles
    base = jnp.minimum(tile // TILE, mask_hbm.shape[1] // TILE - WINDOW // TILE) * TILE
    window = mask_hbm.at[:, pl.ds(pl.multiple_of(base, TILE), WINDOW)]
    return pltpu.make_async_copy(window, mask, sem), tile - base


def block_cols(block):
    return pl.ds(pl.multiple_of(block * TILE, TILE), TILE)


def compress_kernel(tiles, mask_hbm, rows_hbm, out_ref, mask, rows_ref, mask_sem, rows_sem):
    mask_in, origin = mask_copy(mask_hbm, mask, mask_sem, tiles)
    rows_in = pltpu.make_async_copy(rows_hbm, rows_ref, rows_sem)
    mask_in.start()
    rows_in.start()
    mask_in.wait()
    integ = lax.axis_index(INTEG)
    groups = [blocks_of(mask, origin + (integ * ROWS + g * GROUP) // TILE) for g in range(ROWS // GROUP)]
    rows_in.wait()
    for g, (first, second, count) in enumerate(groups):
        rows = pl.ds(g * GROUP, GROUP)
        for half, block in ((0, first), (1, second)):
            part = rows_ref[rows, block_cols(block)]
            out_ref[rows, pl.ds(half * TILE, TILE)] = jnp.where(count > half, part, jnp.zeros_like(part))


def ladder_kernel(tiles, mask_hbm, amp_ref, own_ref, other_ref, out_ref, mask, packed, total, mask_sem):
    mask_in, origin = mask_copy(mask_hbm, mask, mask_sem, tiles)
    mask_in.start()
    core = lax.axis_index("c")
    for slot in range(16):
        rows = pl.ds(slot * ROWS, ROWS)
        for which, ref in ((core, own_ref), (1 - core, other_ref)):
            at = pl.multiple_of((2 * chip_of(slot) + which) * ROWS, GROUP)
            packed[pl.ds(at, ROWS), :] = ref[rows, :]
    mask_in.wait()
    pairs, width = total.shape
    total[...] = jnp.zeros_like(total)
    for tile in range(tiles):
        first, second, _ = blocks_of(mask, origin + tile)
        cols = pl.ds(tile * TILE, TILE)
        part = jnp.dot(amp_ref[:, cols], packed[cols, :], preferred_element_type=jnp.float32)
        total[:, block_cols(first)] += part[:, :TILE]
        total[:, block_cols(second)] += part[:, TILE:]
    largest = jnp.max(jnp.abs(total[...]))
    exponent = jnp.floor(jnp.log2(jnp.maximum(jnp.full((8, TILE), largest), 2.0**-100))) - 10.0
    scale = 0.5 * jnp.exp2(-exponent[:1, :1])
    places, rows = out_ref.shape[0], out_ref.shape[1] // 2
    for place in range(places):
        for zh in range(2):
            piece = total[pl.ds((zh * places + place) * rows, rows), :]
            out_ref[place, pl.ds(zh * rows, rows), :width] = piece * scale
        out_ref[place, :, width:] = exponent


def combine_kernel(parts_ref, mine_ref, theirs_ref, zh_ref):
    rows, width = mine_ref.shape
    total = jnp.zeros((2 * rows, width), jnp.float32)
    for i in range(parts_ref.shape[0]):
        total = total + parts_ref[i, :, :width] * jnp.exp2(parts_ref[i, :, width:])[:, :1]
    zh = lax.axis_index("zh")
    first = zh == 0
    zh_ref[...] = jnp.full(zh_ref.shape, zh, jnp.int32)
    mine_ref[...] = jnp.where(first, total[:rows], total[rows:])
    theirs_ref[...] = jnp.where(first, total[rows:], total[:rows])


def per_device(amplitudes, integrals, block_mask, residual_in):
    cd_tiles, ab_tiles = block_mask.shape
    pairs, width = amplitudes.shape[0], ab_tiles * TILE
    tiles = cd_tiles // lax.axis_size(TASK)
    places = lax.axis_size(PLANE)
    hbm_spec = pl.BlockSpec(memory_space=pltpu.HBM)
    vmem_spec = pl.BlockSpec(memory_space=pltpu.VMEM)
    mask = block_mask.T
    gather = functools.partial(lax.all_gather, axis=0, tiled=True)

    messages = (places, 2 * residual_in.shape[0], width + TILE)
    packed = pl.pallas_call(
        functools.partial(compress_kernel, tiles),
        out_shape=jax.ShapeDtypeStruct((ROWS, 2 * TILE), jnp.bfloat16),
        in_specs=[hbm_spec, hbm_spec],
        out_specs=vmem_spec,
        scratch_shapes=[
            pltpu.SMEM((ab_tiles, WINDOW), jnp.int32),
            pltpu.VMEM(integrals.shape, jnp.bfloat16),
            pltpu.SemaphoreType.DMA,
            pltpu.SemaphoreType.DMA,
        ],
        name="compress",
    )(mask, integrals)
    cores, upper = lax.axis_size("c"), lax.axis_size(("z8", "z4"))
    rings = [[(z * 4 + place) * cores + core for place in RING] for z in range(upper) for core in range(cores)]
    own = gather(gather(gather(packed, "z8"), "z4"), INTEG, axis_index_groups=rings)
    other = lax.ppermute(own, "c", SWAP)
    ladder = pl.pallas_call(
        functools.partial(ladder_kernel, tiles),
        out_shape=jax.ShapeDtypeStruct(messages, jnp.float32),
        in_specs=[hbm_spec] + [vmem_spec] * 3,
        out_specs=vmem_spec,
        scratch_shapes=[
            pltpu.SMEM((ab_tiles, WINDOW), jnp.int32),
            pltpu.VMEM((32 * ROWS, 2 * TILE), jnp.bfloat16),
            pltpu.VMEM((pairs, width), jnp.float32),
            pltpu.SemaphoreType.DMA,
        ],
        compiler_params=pltpu.CompilerParams(vmem_limit_bytes=12 * MIB),
        name="ladder",
    )(mask, amplitudes, own, other)
    parts = lax.all_to_all(ladder.astype(jnp.float16), PLANE, 0, 0, tiled=True)
    mine, theirs, zh = pl.pallas_call(
        combine_kernel,
        out_shape=tuple(jax.ShapeDtypeStruct(residual_in.shape, t) for t in (jnp.float32, jnp.float32, jnp.int32)),
        in_specs=[vmem_spec],
        out_specs=(vmem_spec,) * 3,
        compiler_params=pltpu.CompilerParams(vmem_limit_bytes=4 * MIB),
        name="combine",
    )(parts.astype(jnp.float32))
    both = lax.all_gather(theirs, "zh", axis=0)
    return residual_in + (mine + jnp.where(zh == 0, both[1], both[0]))


def solution(mesh):
    fine = Mesh(mesh.devices.reshape(SIZES), TASK + INTEG)
    return jax.shard_map(
        per_device,
        mesh=fine,
        in_specs=(P(INTEG, TASK), P(TASK + INTEG, None), P(), P(INTEG + TASK, None)),
        out_specs=P(INTEG + TASK, None),
        check_vma=False,
    )
```

```python
import functools

import jax
import jax.numpy as jnp
from jax import lax
from jax.experimental import pallas as pl
from jax.experimental.pallas import tpu as pltpu
from jax.sharding import Mesh
from jax.sharding import PartitionSpec as P

TILE = 128
ROWS = 96
GROUP = 32
TASK = ("zh", "y", "x")
PLANE = ("y", "x")
INTEG = ("z", "c")
SIZES = (2, 4, 4, 16, 2)
SWAP = ((0, 1), (1, 0))
CHIPS = 16
RING = (0, *range(1, CHIPS, 2), *range(CHIPS - 2, 0, -2))
WINDOW = 2 * TILE
MIB = 1024 * 1024


def blocks_of(mask, tile):
    first, second, count = jnp.int32(0), jnp.int32(0), jnp.int32(0)
    for b in range(mask.shape[0]):
        one = mask[b, tile] != 0
        first = jnp.where(one & (count == 0), b, first)
        second = jnp.where(one & (count == 1), b, second)
        count = count + one.astype(jnp.int32)
    return first, second, count


def mask_copy(mask_hbm, mask, sem, tiles):
    tile = lax.axis_index(TASK) * tiles
    base = jnp.minimum(tile // TILE, mask_hbm.shape[1] // TILE - WINDOW // TILE) * TILE
    window = mask_hbm.at[:, pl.ds(pl.multiple_of(base, TILE), WINDOW)]
    return pltpu.make_async_copy(window, mask, sem), tile - base


def block_cols(block):
    return pl.ds(pl.multiple_of(block * TILE, TILE), TILE)


def compress_kernel(tiles, mask_hbm, rows_hbm, out_ref, mask, rows_ref, mask_sem, rows_sem):
    mask_in, origin = mask_copy(mask_hbm, mask, mask_sem, tiles)
    rows_in = pltpu.make_async_copy(rows_hbm, rows_ref, rows_sem)
    mask_in.start()
    rows_in.start()
    mask_in.wait()
    integ = lax.axis_index(INTEG)
    groups = [blocks_of(mask, origin + (integ * ROWS + g * GROUP) // TILE) for g in range(ROWS // GROUP)]
    rows_in.wait()
    for g, (first, second, count) in enumerate(groups):
        rows = pl.ds(g * GROUP, GROUP)
        for half, block in ((0, first), (1, second)):
            part = rows_ref[rows, block_cols(block)]
            out_ref[rows, pl.ds(half * TILE, TILE)] = jnp.where(count > half, part, jnp.zeros_like(part))


def ladder_kernel(tiles, mask_hbm, amp_ref, own_ref, other_ref, out_ref, mask, packed, total, mask_sem):
    mask_in, origin = mask_copy(mask_hbm, mask, mask_sem, tiles)
    mask_in.start()
    core = lax.axis_index("c")
    for slot in range(CHIPS):
        rows = pl.ds(slot * ROWS, ROWS)
        for which, ref in ((core, own_ref), (1 - core, other_ref)):
            at = pl.multiple_of((2 * RING[slot] + which) * ROWS, GROUP)
            packed[pl.ds(at, ROWS), :] = ref[rows, :]
    mask_in.wait()
    pairs, width = total.shape
    total[...] = jnp.zeros_like(total)
    for tile in range(tiles):
        first, second, _ = blocks_of(mask, origin + tile)
        cols = pl.ds(tile * TILE, TILE)
        part = jnp.dot(amp_ref[:, cols], packed[cols, :], preferred_element_type=jnp.float32)
        total[:, block_cols(first)] += part[:, :TILE]
        total[:, block_cols(second)] += part[:, TILE:]
    largest = jnp.max(jnp.abs(total[...]))
    exponent = jnp.floor(jnp.log2(jnp.maximum(jnp.full((8, TILE), largest), 2.0**-100))) - 10.0
    scale = 0.5 * jnp.exp2(-exponent[:1, :1])
    places, rows = out_ref.shape[0], out_ref.shape[1] // 2
    for place in range(places):
        for zh in range(2):
            piece = total[pl.ds((zh * places + place) * rows, rows), :]
            out_ref[place, pl.ds(zh * rows, rows), :width] = piece * scale
        out_ref[place, :, width:] = exponent


def combine_kernel(parts_ref, mine_ref, theirs_ref, zh_ref):
    rows, width = mine_ref.shape
    total = jnp.zeros((2 * rows, width), jnp.float32)
    for i in range(parts_ref.shape[0]):
        total = total + parts_ref[i, :, :width] * jnp.exp2(parts_ref[i, :, width:])[:, :1]
    zh = lax.axis_index("zh")
    first = zh == 0
    zh_ref[...] = jnp.full(zh_ref.shape, zh, jnp.int32)
    mine_ref[...] = jnp.where(first, total[:rows], total[rows:])
    theirs_ref[...] = jnp.where(first, total[rows:], total[:rows])


def per_device(amplitudes, integrals, block_mask, residual_in):
    cd_tiles, ab_tiles = block_mask.shape
    pairs, width = amplitudes.shape[0], ab_tiles * TILE
    tiles = cd_tiles // lax.axis_size(TASK)
    places = lax.axis_size(PLANE)
    hbm_spec = pl.BlockSpec(memory_space=pltpu.HBM)
    vmem_spec = pl.BlockSpec(memory_space=pltpu.VMEM)
    mask = block_mask.T
    messages = (places, 2 * residual_in.shape[0], width + TILE)
    packed = pl.pallas_call(
        functools.partial(compress_kernel, tiles),
        out_shape=jax.ShapeDtypeStruct((ROWS, 2 * TILE), jnp.bfloat16),
        in_specs=[hbm_spec, hbm_spec],
        out_specs=vmem_spec,
        scratch_shapes=[
            pltpu.SMEM((ab_tiles, WINDOW), jnp.int32),
            pltpu.VMEM(integrals.shape, jnp.bfloat16),
            pltpu.SemaphoreType.DMA,
            pltpu.SemaphoreType.DMA,
        ],
        name="compress",
    )(mask, integrals)
    cores = lax.axis_size("c")
    rings = [[chip * cores + core for chip in RING] for core in range(cores)]
    own = lax.all_gather(packed, INTEG, axis=0, tiled=True, axis_index_groups=rings)
    other = lax.ppermute(own, "c", SWAP)
    ladder = pl.pallas_call(
        functools.partial(ladder_kernel, tiles),
        out_shape=jax.ShapeDtypeStruct(messages, jnp.float32),
        in_specs=[hbm_spec] + [vmem_spec] * 3,
        out_specs=vmem_spec,
        scratch_shapes=[
            pltpu.SMEM((ab_tiles, WINDOW), jnp.int32),
            pltpu.VMEM((32 * ROWS, 2 * TILE), jnp.bfloat16),
            pltpu.VMEM((pairs, width), jnp.float32),
            pltpu.SemaphoreType.DMA,
        ],
        compiler_params=pltpu.CompilerParams(vmem_limit_bytes=12 * MIB),
        name="ladder",
    )(mask, amplitudes, own, other)
    parts = lax.all_to_all(ladder.astype(jnp.float16), PLANE, 0, 0, tiled=True)
    mine, theirs, zh = pl.pallas_call(
        combine_kernel,
        out_shape=tuple(jax.ShapeDtypeStruct(residual_in.shape, t) for t in (jnp.float32, jnp.float32, jnp.int32)),
        in_specs=[vmem_spec],
        out_specs=(vmem_spec,) * 3,
        compiler_params=pltpu.CompilerParams(vmem_limit_bytes=4 * MIB),
        name="combine",
    )(parts.astype(jnp.float32))
    both = lax.all_gather(theirs, "zh", axis=0)
    return residual_in + (mine + jnp.where(zh == 0, both[1], both[0]))


def solution(mesh):
    fine = Mesh(mesh.devices.reshape(SIZES), TASK + INTEG)
    return jax.shard_map(
        per_device,
        mesh=fine,
        in_specs=(P(INTEG, TASK), P(TASK + INTEG, None), P(), P(INTEG + TASK, None)),
        out_specs=P(INTEG + TASK, None),
        check_vma=False,
    )
```

```python
import functools

import jax
import jax.numpy as jnp
from jax import lax
from jax.experimental import pallas as pl
from jax.experimental.pallas import tpu as pltpu
from jax.sharding import Mesh
from jax.sharding import PartitionSpec as P

TILE = 128
ROWS = 96
GROUP = 32
TASK = ("zh", "y", "x")
PLANE = ("y", "x")
INTEG = ("z", "c")
SIZES = (2, 4, 4, 16, 2)
SWAP = ((0, 1), (1, 0))
CHIPS = 16
RING = (0, *range(1, CHIPS, 2), *range(CHIPS - 2, 0, -2))
RINGS = (RING, RING[::-1])
WINDOW = 2 * TILE
MIB = 1024 * 1024


def blocks_of(mask, tile):
    first, second, count = jnp.int32(0), jnp.int32(0), jnp.int32(0)
    for b in range(mask.shape[0]):
        one = mask[b, tile] != 0
        first = jnp.where(one & (count == 0), b, first)
        second = jnp.where(one & (count == 1), b, second)
        count = count + one.astype(jnp.int32)
    return first, second, count


def mask_copy(mask_hbm, mask, sem, tiles):
    tile = lax.axis_index(TASK) * tiles
    base = jnp.minimum(tile // TILE, mask_hbm.shape[1] // TILE - WINDOW // TILE) * TILE
    window = mask_hbm.at[:, pl.ds(pl.multiple_of(base, TILE), WINDOW)]
    return pltpu.make_async_copy(window, mask, sem), tile - base


def block_cols(block):
    return pl.ds(pl.multiple_of(block * TILE, TILE), TILE)


def compress_kernel(tiles, mask_hbm, rows_hbm, out_ref, mask, rows_ref, mask_sem, rows_sem):
    mask_in, origin = mask_copy(mask_hbm, mask, mask_sem, tiles)
    rows_in = pltpu.make_async_copy(rows_hbm, rows_ref, rows_sem)
    mask_in.start()
    rows_in.start()
    mask_in.wait()
    integ = lax.axis_index(INTEG)
    groups = [blocks_of(mask, origin + (integ * ROWS + g * GROUP) // TILE) for g in range(ROWS // GROUP)]
    rows_in.wait()
    for g, (first, second, count) in enumerate(groups):
        rows = pl.ds(g * GROUP, GROUP)
        for half, block in ((0, first), (1, second)):
            part = rows_ref[rows, block_cols(block)]
            out_ref[rows, pl.ds(half * TILE, TILE)] = jnp.where(count > half, part, jnp.zeros_like(part))


def ladder_kernel(tiles, mask_hbm, amp_ref, own_ref, other_ref, out_ref, mask, packed, total, mask_sem):
    mask_in, origin = mask_copy(mask_hbm, mask, mask_sem, tiles)
    mask_in.start()
    core = lax.axis_index("c")
    for slot in range(CHIPS):
        rows = pl.ds(slot * ROWS, ROWS)
        for which, ref in ((core, own_ref), (1 - core, other_ref)):
            chip = jnp.where(which == 0, RINGS[0][slot], RINGS[1][slot])
            at = pl.multiple_of((2 * chip + which) * ROWS, GROUP)
            packed[pl.ds(at, ROWS), :] = ref[rows, :]
    mask_in.wait()
    pairs, width = total.shape
    total[...] = jnp.zeros_like(total)
    for tile in range(tiles):
        first, second, _ = blocks_of(mask, origin + tile)
        cols = pl.ds(tile * TILE, TILE)
        part = jnp.dot(amp_ref[:, cols], packed[cols, :], preferred_element_type=jnp.float32)
        total[:, block_cols(first)] += part[:, :TILE]
        total[:, block_cols(second)] += part[:, TILE:]
    largest = jnp.max(jnp.abs(total[...]))
    exponent = jnp.floor(jnp.log2(jnp.maximum(jnp.full((8, TILE), largest), 2.0**-100))) - 10.0
    scale = 0.5 * jnp.exp2(-exponent[:1, :1])
    places, rows = out_ref.shape[0], out_ref.shape[1] // 2
    for place in range(places):
        for zh in range(2):
            piece = total[pl.ds((zh * places + place) * rows, rows), :]
            out_ref[place, pl.ds(zh * rows, rows), :width] = piece * scale
        out_ref[place, :, width:] = exponent


def combine_kernel(parts_ref, mine_ref, theirs_ref, zh_ref):
    rows, width = mine_ref.shape
    total = jnp.zeros((2 * rows, width), jnp.float32)
    for i in range(parts_ref.shape[0]):
        total = total + parts_ref[i, :, :width] * jnp.exp2(parts_ref[i, :, width:])[:, :1]
    zh = lax.axis_index("zh")
    first = zh == 0
    zh_ref[...] = jnp.full(zh_ref.shape, zh, jnp.int32)
    mine_ref[...] = jnp.where(first, total[:rows], total[rows:])
    theirs_ref[...] = jnp.where(first, total[rows:], total[:rows])


def per_device(amplitudes, integrals, block_mask, residual_in):
    cd_tiles, ab_tiles = block_mask.shape
    pairs, width = amplitudes.shape[0], ab_tiles * TILE
    tiles = cd_tiles // lax.axis_size(TASK)
    places = lax.axis_size(PLANE)
    hbm_spec = pl.BlockSpec(memory_space=pltpu.HBM)
    vmem_spec = pl.BlockSpec(memory_space=pltpu.VMEM)
    mask = block_mask.T
    messages = (places, 2 * residual_in.shape[0], width + TILE)
    packed = pl.pallas_call(
        functools.partial(compress_kernel, tiles),
        out_shape=jax.ShapeDtypeStruct((ROWS, 2 * TILE), jnp.bfloat16),
        in_specs=[hbm_spec, hbm_spec],
        out_specs=vmem_spec,
        scratch_shapes=[
            pltpu.SMEM((ab_tiles, WINDOW), jnp.int32),
            pltpu.VMEM(integrals.shape, jnp.bfloat16),
            pltpu.SemaphoreType.DMA,
            pltpu.SemaphoreType.DMA,
        ],
        name="compress",
    )(mask, integrals)
    cores = lax.axis_size("c")
    rings = [[chip * cores + core for chip in ring] for core, ring in enumerate(RINGS)]
    own = lax.all_gather(packed, INTEG, axis=0, tiled=True, axis_index_groups=rings)
    other = lax.ppermute(own, "c", SWAP)
    ladder = pl.pallas_call(
        functools.partial(ladder_kernel, tiles),
        out_shape=jax.ShapeDtypeStruct(messages, jnp.float32),
        in_specs=[hbm_spec] + [vmem_spec] * 3,
        out_specs=vmem_spec,
        scratch_shapes=[
            pltpu.SMEM((ab_tiles, WINDOW), jnp.int32),
            pltpu.VMEM((32 * ROWS, 2 * TILE), jnp.bfloat16),
            pltpu.VMEM((pairs, width), jnp.float32),
            pltpu.SemaphoreType.DMA,
        ],
        compiler_params=pltpu.CompilerParams(vmem_limit_bytes=12 * MIB),
        name="ladder",
    )(mask, amplitudes, own, other)
    parts = lax.all_to_all(ladder.astype(jnp.float16), PLANE, 0, 0, tiled=True)
    mine, theirs, zh = pl.pallas_call(
        combine_kernel,
        out_shape=tuple(jax.ShapeDtypeStruct(residual_in.shape, t) for t in (jnp.float32, jnp.float32, jnp.int32)),
        in_specs=[vmem_spec],
        out_specs=(vmem_spec,) * 3,
        compiler_params=pltpu.CompilerParams(vmem_limit_bytes=4 * MIB),
        name="combine",
    )(parts.astype(jnp.float32))
    both = lax.all_gather(theirs, "zh", axis=0)
    return residual_in + (mine + jnp.where(zh == 0, both[1], both[0]))


def solution(mesh):
    fine = Mesh(mesh.devices.reshape(SIZES), TASK + INTEG)
    return jax.shard_map(
        per_device,
        mesh=fine,
        in_specs=(P(INTEG, TASK), P(TASK + INTEG, None), P(), P(INTEG + TASK, None)),
        out_specs=P(INTEG + TASK, None),
        check_vma=False,
    )
```

```python
import functools

import jax
import jax.numpy as jnp
from jax import lax
from jax.experimental import pallas as pl
from jax.experimental.pallas import tpu as pltpu
from jax.sharding import Mesh
from jax.sharding import PartitionSpec as P

TILE = 128
ROWS = 96
GROUP = 32
TASK = ("zh", "y", "x")
PLANE = ("y", "x")
INTEG = ("z", "c")
SIZES = (2, 4, 4, 16, 2)
SWAP = ((0, 1), (1, 0))
CHIPS = 16
RING = (0, *range(1, CHIPS, 2), *range(CHIPS - 2, 0, -2))
SNAKE = tuple(4 * y + (x if y % 2 == 0 else 3 - x) for y in range(4) for x in range(4))
WINDOW = 2 * TILE
MIB = 1024 * 1024


def blocks_of(mask, tile):
    first, second, count = jnp.int32(0), jnp.int32(0), jnp.int32(0)
    for b in range(mask.shape[0]):
        one = mask[b, tile] != 0
        first = jnp.where(one & (count == 0), b, first)
        second = jnp.where(one & (count == 1), b, second)
        count = count + one.astype(jnp.int32)
    return first, second, count


def mask_copy(mask_hbm, mask, sem, tiles):
    tile = lax.axis_index(TASK) * tiles
    base = jnp.minimum(tile // TILE, mask_hbm.shape[1] // TILE - WINDOW // TILE) * TILE
    window = mask_hbm.at[:, pl.ds(pl.multiple_of(base, TILE), WINDOW)]
    return pltpu.make_async_copy(window, mask, sem), tile - base


def block_cols(block):
    return pl.ds(pl.multiple_of(block * TILE, TILE), TILE)


def compress_kernel(tiles, mask_hbm, rows_hbm, out_ref, mask, rows_ref, mask_sem, rows_sem):
    mask_in, origin = mask_copy(mask_hbm, mask, mask_sem, tiles)
    rows_in = pltpu.make_async_copy(rows_hbm, rows_ref, rows_sem)
    mask_in.start()
    rows_in.start()
    mask_in.wait()
    integ = lax.axis_index(INTEG)
    groups = [blocks_of(mask, origin + (integ * ROWS + g * GROUP) // TILE) for g in range(ROWS // GROUP)]
    rows_in.wait()
    for g, (first, second, count) in enumerate(groups):
        rows = pl.ds(g * GROUP, GROUP)
        for half, block in ((0, first), (1, second)):
            part = rows_ref[rows, block_cols(block)]
            out_ref[rows, pl.ds(half * TILE, TILE)] = jnp.where(count > half, part, jnp.zeros_like(part))


def ladder_kernel(tiles, mask_hbm, amp_ref, own_ref, other_ref, out_ref, mask, packed, total, mask_sem):
    mask_in, origin = mask_copy(mask_hbm, mask, mask_sem, tiles)
    mask_in.start()
    core = lax.axis_index("c")
    for slot in range(CHIPS):
        rows = pl.ds(slot * ROWS, ROWS)
        for which, ref in ((core, own_ref), (1 - core, other_ref)):
            at = pl.multiple_of((2 * RING[slot] + which) * ROWS, GROUP)
            packed[pl.ds(at, ROWS), :] = ref[rows, :]
    mask_in.wait()
    pairs, width = total.shape
    total[...] = jnp.zeros_like(total)
    for tile in range(tiles):
        first, second, _ = blocks_of(mask, origin + tile)
        cols = pl.ds(tile * TILE, TILE)
        part = jnp.dot(amp_ref[:, cols], packed[cols, :], preferred_element_type=jnp.float32)
        total[:, block_cols(first)] += part[:, :TILE]
        total[:, block_cols(second)] += part[:, TILE:]
    largest = jnp.max(jnp.abs(total[...]))
    exponent = jnp.floor(jnp.log2(jnp.maximum(jnp.full((8, TILE), largest), 2.0**-100))) - 10.0
    scale = 0.5 * jnp.exp2(-exponent[:1, :1])
    places, rows = out_ref.shape[0], out_ref.shape[1] // 2
    for slot, place in enumerate(SNAKE):
        for zh in range(2):
            piece = total[pl.ds((zh * places + place) * rows, rows), :]
            out_ref[slot, pl.ds(zh * rows, rows), :width] = piece * scale
        out_ref[slot, :, width:] = exponent


def combine_kernel(parts_ref, mine_ref, theirs_ref, zh_ref):
    rows, width = mine_ref.shape
    total = jnp.zeros((2 * rows, width), jnp.float32)
    for i in range(parts_ref.shape[0]):
        total = total + parts_ref[i, :, :width] * jnp.exp2(parts_ref[i, :, width:])[:, :1]
    zh = lax.axis_index("zh")
    first = zh == 0
    zh_ref[...] = jnp.full(zh_ref.shape, zh, jnp.int32)
    mine_ref[...] = jnp.where(first, total[:rows], total[rows:])
    theirs_ref[...] = jnp.where(first, total[rows:], total[:rows])


def per_device(amplitudes, integrals, block_mask, residual_in):
    cd_tiles, ab_tiles = block_mask.shape
    pairs, width = amplitudes.shape[0], ab_tiles * TILE
    tiles = cd_tiles // lax.axis_size(TASK)
    places = lax.axis_size(PLANE)
    hbm_spec = pl.BlockSpec(memory_space=pltpu.HBM)
    vmem_spec = pl.BlockSpec(memory_space=pltpu.VMEM)
    mask = block_mask.T
    messages = (places, 2 * residual_in.shape[0], width + TILE)
    packed = pl.pallas_call(
        functools.partial(compress_kernel, tiles),
        out_shape=jax.ShapeDtypeStruct((ROWS, 2 * TILE), jnp.bfloat16),
        in_specs=[hbm_spec, hbm_spec],
        out_specs=vmem_spec,
        scratch_shapes=[
            pltpu.SMEM((ab_tiles, WINDOW), jnp.int32),
            pltpu.VMEM(integrals.shape, jnp.bfloat16),
            pltpu.SemaphoreType.DMA,
            pltpu.SemaphoreType.DMA,
        ],
        name="compress",
    )(mask, integrals)
    cores = lax.axis_size("c")
    rings = [[chip * cores + core for chip in RING] for core in range(cores)]
    own = lax.all_gather(packed, INTEG, axis=0, tiled=True, axis_index_groups=rings)
    other = lax.ppermute(own, "c", SWAP)
    ladder = pl.pallas_call(
        functools.partial(ladder_kernel, tiles),
        out_shape=jax.ShapeDtypeStruct(messages, jnp.float32),
        in_specs=[hbm_spec] + [vmem_spec] * 3,
        out_specs=vmem_spec,
        scratch_shapes=[
            pltpu.SMEM((ab_tiles, WINDOW), jnp.int32),
            pltpu.VMEM((32 * ROWS, 2 * TILE), jnp.bfloat16),
            pltpu.VMEM((pairs, width), jnp.float32),
            pltpu.SemaphoreType.DMA,
        ],
        compiler_params=pltpu.CompilerParams(vmem_limit_bytes=12 * MIB),
        name="ladder",
    )(mask, amplitudes, own, other)
    parts = lax.all_to_all(ladder.astype(jnp.float16), PLANE, 0, 0, tiled=True, axis_index_groups=[SNAKE])
    mine, theirs, zh = pl.pallas_call(
        combine_kernel,
        out_shape=tuple(jax.ShapeDtypeStruct(residual_in.shape, t) for t in (jnp.float32, jnp.float32, jnp.int32)),
        in_specs=[vmem_spec],
        out_specs=(vmem_spec,) * 3,
        compiler_params=pltpu.CompilerParams(vmem_limit_bytes=4 * MIB),
        name="combine",
    )(parts.astype(jnp.float32))
    both = lax.all_gather(theirs, "zh", axis=0)
    return residual_in + (mine + jnp.where(zh == 0, both[1], both[0]))


def solution(mesh):
    fine = Mesh(mesh.devices.reshape(SIZES), TASK + INTEG)
    return jax.shard_map(
        per_device,
        mesh=fine,
        in_specs=(P(INTEG, TASK), P(TASK + INTEG, None), P(), P(INTEG + TASK, None)),
        out_specs=P(INTEG + TASK, None),
        check_vma=False,
    )
```

```python
import functools

import jax
import jax.numpy as jnp
from jax import lax
from jax.experimental import pallas as pl
from jax.experimental.pallas import tpu as pltpu
from jax.sharding import Mesh
from jax.sharding import PartitionSpec as P

TILE = 128
ROWS = 96
GROUP = 32
TASK = ("zh", "y", "x")
PLANE = ("y", "x")
INTEG = ("z", "c")
SIZES = (2, 4, 4, 16, 2)
SWAP = ((0, 1), (1, 0))
CHIPS = 16
RING = (0, *range(1, CHIPS, 2), *range(CHIPS - 2, 0, -2))
WINDOW = 2 * TILE
MIB = 1024 * 1024


def blocks_of(mask, tile):
    first, second, count = jnp.int32(0), jnp.int32(0), jnp.int32(0)
    for b in range(mask.shape[0]):
        one = mask[b, tile] != 0
        first = jnp.where(one & (count == 0), b, first)
        second = jnp.where(one & (count == 1), b, second)
        count = count + one.astype(jnp.int32)
    return first, second, count


def mask_copy(mask_hbm, mask, sem, tiles):
    tile = lax.axis_index(TASK) * tiles
    base = jnp.minimum(tile // TILE, mask_hbm.shape[1] // TILE - WINDOW // TILE) * TILE
    window = mask_hbm.at[:, pl.ds(pl.multiple_of(base, TILE), WINDOW)]
    return pltpu.make_async_copy(window, mask, sem), tile - base


def block_cols(block):
    return pl.ds(pl.multiple_of(block * TILE, TILE), TILE)


def compress_kernel(tiles, mask_hbm, rows_hbm, out_ref, mask, rows_ref, mask_sem, rows_sem):
    mask_in, origin = mask_copy(mask_hbm, mask, mask_sem, tiles)
    rows_in = pltpu.make_async_copy(rows_hbm, rows_ref, rows_sem)
    mask_in.start()
    rows_in.start()
    mask_in.wait()
    integ = lax.axis_index(INTEG)
    groups = [blocks_of(mask, origin + (integ * ROWS + g * GROUP) // TILE) for g in range(ROWS // GROUP)]
    rows_in.wait()
    for g, (first, second, count) in enumerate(groups):
        rows = pl.ds(g * GROUP, GROUP)
        for half, block in ((0, first), (1, second)):
            part = rows_ref[rows, block_cols(block)]
            out_ref[rows, pl.ds(half * TILE, TILE)] = jnp.where(count > half, part, jnp.zeros_like(part))


def put_rows(which, rows_ref, packed):
    for slot in range(CHIPS):
        at = pl.multiple_of((2 * RING[slot] + which) * ROWS, GROUP)
        packed[pl.ds(at, ROWS), :] = rows_ref[pl.ds(slot * ROWS, ROWS), :]


def place_kernel(own_ref, packed):
    put_rows(lax.axis_index("c"), own_ref, packed)


def ladder_kernel(tiles, mask_hbm, amp_ref, placed_ref, other_ref, out_ref, packed, mask, total, mask_sem):
    mask_in, origin = mask_copy(mask_hbm, mask, mask_sem, tiles)
    mask_in.start()
    put_rows(1 - lax.axis_index("c"), other_ref, packed)
    mask_in.wait()
    pairs, width = total.shape
    total[...] = jnp.zeros_like(total)
    for tile in range(tiles):
        first, second, _ = blocks_of(mask, origin + tile)
        cols = pl.ds(tile * TILE, TILE)
        part = jnp.dot(amp_ref[:, cols], packed[cols, :], preferred_element_type=jnp.float32)
        total[:, block_cols(first)] += part[:, :TILE]
        total[:, block_cols(second)] += part[:, TILE:]
    largest = jnp.max(jnp.abs(total[...]))
    exponent = jnp.floor(jnp.log2(jnp.maximum(jnp.full((8, TILE), largest), 2.0**-100))) - 10.0
    scale = 0.5 * jnp.exp2(-exponent[:1, :1])
    places, rows = out_ref.shape[0], out_ref.shape[1] // 2
    for place in range(places):
        for zh in range(2):
            piece = total[pl.ds((zh * places + place) * rows, rows), :]
            out_ref[place, pl.ds(zh * rows, rows), :width] = piece * scale
        out_ref[place, :, width:] = exponent


def combine_kernel(parts_ref, mine_ref, theirs_ref, zh_ref):
    rows, width = mine_ref.shape
    total = jnp.zeros((2 * rows, width), jnp.float32)
    for i in range(parts_ref.shape[0]):
        total = total + parts_ref[i, :, :width] * jnp.exp2(parts_ref[i, :, width:])[:, :1]
    zh = lax.axis_index("zh")
    first = zh == 0
    zh_ref[...] = jnp.full(zh_ref.shape, zh, jnp.int32)
    mine_ref[...] = jnp.where(first, total[:rows], total[rows:])
    theirs_ref[...] = jnp.where(first, total[rows:], total[:rows])


def per_device(amplitudes, integrals, block_mask, residual_in):
    cd_tiles, ab_tiles = block_mask.shape
    pairs, width = amplitudes.shape[0], ab_tiles * TILE
    tiles = cd_tiles // lax.axis_size(TASK)
    places = lax.axis_size(PLANE)
    hbm_spec = pl.BlockSpec(memory_space=pltpu.HBM)
    vmem_spec = pl.BlockSpec(memory_space=pltpu.VMEM)
    mask = block_mask.T
    messages = (places, 2 * residual_in.shape[0], width + TILE)
    packed = pl.pallas_call(
        functools.partial(compress_kernel, tiles),
        out_shape=jax.ShapeDtypeStruct((ROWS, 2 * TILE), jnp.bfloat16),
        in_specs=[hbm_spec, hbm_spec],
        out_specs=vmem_spec,
        scratch_shapes=[
            pltpu.SMEM((ab_tiles, WINDOW), jnp.int32),
            pltpu.VMEM(integrals.shape, jnp.bfloat16),
            pltpu.SemaphoreType.DMA,
            pltpu.SemaphoreType.DMA,
        ],
        name="compress",
    )(mask, integrals)
    cores = lax.axis_size("c")
    rings = [[chip * cores + core for chip in RING] for core in range(cores)]
    own = lax.all_gather(packed, INTEG, axis=0, tiled=True, axis_index_groups=rings)
    other = lax.ppermute(own, "c", SWAP)
    gathered = jax.ShapeDtypeStruct((2 * own.shape[0], own.shape[1]), own.dtype)
    placed = pl.pallas_call(
        place_kernel,
        out_shape=gathered,
        in_specs=[vmem_spec],
        out_specs=vmem_spec,
        compiler_params=pltpu.CompilerParams(vmem_limit_bytes=4 * MIB),
        cost_estimate=pl.CostEstimate(flops=0, bytes_accessed=4 * own.size, transcendentals=0),
        name="place",
    )(own)
    ladder, _ = pl.pallas_call(
        functools.partial(ladder_kernel, tiles),
        out_shape=(jax.ShapeDtypeStruct(messages, jnp.float32), gathered),
        in_specs=[hbm_spec] + [vmem_spec] * 3,
        out_specs=(vmem_spec, vmem_spec),
        input_output_aliases={2: 1},
        scratch_shapes=[
            pltpu.SMEM((ab_tiles, WINDOW), jnp.int32),
            pltpu.VMEM((pairs, width), jnp.float32),
            pltpu.SemaphoreType.DMA,
        ],
        compiler_params=pltpu.CompilerParams(vmem_limit_bytes=12 * MIB),
        name="ladder",
    )(mask, amplitudes, placed, other)
    parts = lax.all_to_all(ladder.astype(jnp.float16), PLANE, 0, 0, tiled=True)
    mine, theirs, zh = pl.pallas_call(
        combine_kernel,
        out_shape=tuple(jax.ShapeDtypeStruct(residual_in.shape, t) for t in (jnp.float32, jnp.float32, jnp.int32)),
        in_specs=[vmem_spec],
        out_specs=(vmem_spec,) * 3,
        compiler_params=pltpu.CompilerParams(vmem_limit_bytes=4 * MIB),
        name="combine",
    )(parts.astype(jnp.float32))
    both = lax.all_gather(theirs, "zh", axis=0)
    return residual_in + (mine + jnp.where(zh == 0, both[1], both[0]))


def solution(mesh):
    fine = Mesh(mesh.devices.reshape(SIZES), TASK + INTEG)
    return jax.shard_map(
        per_device,
        mesh=fine,
        in_specs=(P(INTEG, TASK), P(TASK + INTEG, None), P(), P(INTEG + TASK, None)),
        out_specs=P(INTEG + TASK, None),
        check_vma=False,
    )
```
